32 devices in a mesh: groups: 1, rows: 16 (over z, y, x), cols: 2 (over core).
Axes of the slice: x: 2, y: 2, z: 4, core: 2. Of those that a mesh axis runs over, the one named last changes fastest.
Arguments:
- pool_acts: bfloat16 [6144, 1536], P(('groups', 'rows'), 'cols'), may hold values from -1 to 1
- pool_grads: bfloat16 [6144, 4096], P(('groups', 'rows'), 'cols'), may hold values from -0.75 to 0.75
- label_acts: bfloat16 [256, 1536], P(('groups', 'rows'), 'cols'), may hold values from -1 to 1
- label_grads: bfloat16 [256, 4096], P(('groups', 'rows'), 'cols'), may hold values from -0.75 to 0.75
Outputs:
- ntk: float32 [6144, 2, 128], P(('groups', 'rows'), 'cols')
The draws below stay inside these ranges and needn't reach their ends.
All inputs are finite; a program needn't handle non-finite values.
Results may differ from the reference program's by a relative error of at most 0.0003.
Values may be sent and summed in bfloat16 or wider, within the bound.
A program may use at most 64 MiB of HBM per device.

```python
import jax
import jax.numpy as jnp

FF = 1536
D = 4096
LBK = 16
POOL = 6144
LAB = 256
N_ROWS = 16
N_COLS = 2


def block_scale(key, shape, cuts, low, high):
    level = 1.0
    for axis_at, shards_of in cuts:
        draws = jax.random.uniform(jax.random.fold_in(jax.random.fold_in(key, 6), axis_at), (shards_of,), jnp.float32, low / len(cuts), high / len(cuts))
        level = level * jnp.repeat(jnp.exp(draws), shape[axis_at] // shards_of).reshape((-1,) + (1,) * (len(shape) - 1 - axis_at))
    return level


def bell_draw(own_key, shape, spread, bound, pieces=(), dtype=jnp.bfloat16):
    drawn = jax.random.normal(own_key, shape, jnp.float32) * spread
    if len(pieces) > 0:
        drawn = block_scale(own_key, shape, pieces, -0.22, 0.18) * drawn
    return jnp.clip(drawn, min=-bound, max=bound).astype(dtype)


def setup_inputs(seed: int = 0, part: int = 0) -> dict:
    keys = jax.random.split(jax.random.key(seed), 5)
    part_keys = jax.random.split(jax.random.fold_in(keys[4], part), 5)
    pool_acts = bell_draw(part_keys[0], (POOL, FF), (FF ** -0.25), 1.0, ((0, 16), (1, 2)))
    pool_grads = bell_draw(part_keys[1], (POOL, D), (D ** -0.25), 0.75, ((0, 16), (1, 2)))
    label_acts = bell_draw(part_keys[2], (LAB, FF), (FF ** -0.25), 1.0, ((0, 16), (1, 2)))
    label_grads = bell_draw(part_keys[3], (LAB, D), (D ** -0.25), 0.75, ((0, 16), (1, 2)))
    return dict(pool_acts=pool_acts, pool_grads=pool_grads, label_acts=label_acts, label_grads=label_grads)


def reference(pool_acts, pool_grads, label_acts, label_grads):
    acts_gram = jnp.dot(pool_acts, label_acts.T, preferred_element_type=jnp.float32)
    grad_gram = jnp.dot(pool_grads, label_grads.T, preferred_element_type=jnp.float32)
    kernel = acts_gram * grad_gram
    half_len = LBK // N_COLS
    kernel = kernel.reshape(POOL, N_ROWS, N_COLS, half_len)
    kernel = jnp.transpose(kernel, (0, 2, 1, 3))
    return kernel.reshape(POOL, N_COLS, N_ROWS * half_len)
```

```python
import functools

import jax
import jax.numpy as jnp
from jax import lax
from jax.experimental import pallas as pl
from jax.experimental.pallas import tpu as pltpu
from jax.sharding import PartitionSpec as P

MESH = pl.DeviceIdType.MESH
ORDERS = ((0, 2, 1), (0, 1, 2), (2, 0, 1), (1, 0, 2))
LANES = 128


def contract(left, right):
    return lax.dot_general(
        left, right, (((1,), (1,)), ((), ())), preferred_element_type=jnp.float32
    )


def kernel(
    sizes, spans,
    pool_acts, pool_grads, label_acts, label_grads, out_ref,
    buf0, buf1, buf2, buf3, acts, grads, gram, other,
    send_sem, recv_sem, local_sem, pair_send, pair_recv,
):
    bufs = (buf0, buf1, buf2, buf3)
    me = lax.axis_index("rows")
    core = lax.axis_index("cols")
    strides = (sizes[1] * sizes[2], sizes[2], 1)
    place = [lax.rem(me // s, n) for s, n in zip(strides, sizes)]
    blocks = sizes[0] * sizes[1] * sizes[2]

    def at(delta):
        return sum(
            lax.rem(place[a] + delta[a], sizes[a]) * strides[a] for a in range(3)
        )

    def along(axis):
        return [
            tuple(d if a == axis else 0 for a in range(3))
            for d in range(1, sizes[axis])
        ]

    barrier = pltpu.get_barrier_semaphore()
    greeted = 1
    pl.semaphore_signal(
        barrier, inc=1, device_id={"cols": 1 - core}, device_id_type=MESH
    )
    for axis in range(3):
        for peer in along(axis):
            pl.semaphore_signal(
                barrier, inc=1, device_id={"rows": at(peer)}, device_id_type=MESH
            )
            greeted += 1
    pl.semaphore_wait(barrier, greeted)

    own = [label_acts if s is None else label_grads.at[:, s[0] : s[1]] for s in spans]
    sent = []

    def send(k, delta, peer):
        block = at(delta)
        src = bufs[k].at[block] if any(delta) else own[k]
        copy = pltpu.make_async_remote_copy(
            src_ref=src,
            dst_ref=bufs[k].at[block],
            send_sem=send_sem.at[len(sent)],
            recv_sem=recv_sem.at[k, block],
            device_id={"rows": at(peer)},
            device_id_type=MESH,
        )
        copy.start()
        sent.append(copy)

    def arrived(k, delta):
        block = at(delta)
        pltpu.make_async_remote_copy(
            src_ref=bufs[k].at[block],
            dst_ref=bufs[k].at[block],
            send_sem=send_sem.at[0],
            recv_sem=recv_sem.at[k, block],
            device_id={"rows": at(along(2)[0])},
            device_id_type=MESH,
        ).wait_recv()

    def plus(*deltas):
        return tuple(sum(d) for d in zip(*deltas))

    zero = (0, 0, 0)
    for leg in range(3):
        for k, order in enumerate(ORDERS):
            for peer in along(order[leg]):
                send(k, zero, peer)

    local = [
        pltpu.make_async_copy(own[k], bufs[k].at[me], local_sem.at[k])
        for k in range(4)
    ]
    local.append(pltpu.make_async_copy(pool_acts, acts, local_sem.at[4]))
    local.append(pltpu.make_async_copy(pool_grads, grads, local_sem.at[5]))
    for copy in local:
        copy.start()

    for step in range(max(sizes) - 1):
        for k, order in enumerate(ORDERS):
            first = along(order[0])
            if step < len(first):
                arrived(k, first[step])
                for leg in (1, 2):
                    for peer in along(order[leg]):
                        send(k, first[step], peer)

    second = [
        [plus(f, s) for f in [zero] + along(o[0]) for s in along(o[1])]
        for o in ORDERS
    ]
    for step in range(max(len(s) for s in second)):
        for k, order in enumerate(ORDERS):
            if step < len(second[k]):
                arrived(k, second[k][step])
                for peer in along(order[2]):
                    send(k, second[k][step], peer)

    third = [
        [
            plus(f, s, t)
            for f in [zero] + along(o[0])
            for s in [zero] + along(o[1])
            for t in along(o[2])
        ]
        for o in ORDERS
    ]

    def pair(which):
        return pltpu.make_async_remote_copy(
            src_ref=gram.at[which, :, 1 - core],
            dst_ref=other.at[which],
            send_sem=pair_send.at[which],
            recv_sem=pair_recv.at[which],
            device_id={"cols": 1 - core},
            device_id_type=MESH,
        )

    def flat(k):
        return bufs[k][...].reshape(blocks * bufs[k].shape[1], bufs[k].shape[2])

    for copy in local:
        copy.wait()
    for delta in third[0]:
        arrived(0, delta)
    gram[0] = contract(flat(0), acts[...]).reshape(gram.shape[1:])
    pair(0).start()
    for k in (1, 2, 3):
        for delta in third[k]:
            arrived(k, delta)
    total = None
    for k in (1, 2, 3):
        part = contract(flat(k), grads[:, spans[k][0] : spans[k][1]])
        total = part if total is None else total + part
    gram[1] = total.reshape(gram.shape[1:])
    pair(1).start()
    pair(0).wait()
    pair(1).wait()
    result = (gram[0, :, core] + other[0]) * (gram[1, :, core] + other[1])
    out_ref[...] = result.reshape(out_ref.shape[1], out_ref.shape[0]).T
    for copy in sent:
        copy.wait_send()


def body(pool_acts, pool_grads, label_acts, label_grads):
    blocks = lax.axis_size("rows")
    cols = lax.axis_size("cols")
    sizes = (blocks // 4, 2, 2)
    pool_rows = pool_acts.shape[0]
    block_rows = label_acts.shape[0]
    half = block_rows // cols
    wide = label_grads.shape[1]
    quarter = wide // 4
    spans = (None, (0, 2 * quarter), (2 * quarter, 3 * quarter), (3 * quarter, wide))
    widths = (label_acts.shape[1], 2 * quarter, quarter, wide - 3 * quarter)
    sends = 0
    for o in ORDERS:
        n = [sizes[a] for a in o]
        sends += (n[0] - 1) + n[0] * (n[1] - 1) + n[0] * n[1] * (n[2] - 1)
    out = pl.pallas_call(
        functools.partial(kernel, sizes, spans),
        out_shape=jax.ShapeDtypeStruct((pool_rows, blocks * half), jnp.float32),
        in_specs=[pl.BlockSpec(memory_space=pltpu.HBM)] * 4,
        out_specs=pl.BlockSpec(memory_space=pltpu.VMEM),
        scratch_shapes=[
            pltpu.VMEM((blocks, block_rows, w), jnp.bfloat16) for w in widths
        ]
        + [
            pltpu.VMEM(pool_acts.shape, jnp.bfloat16),
            pltpu.VMEM(pool_grads.shape, jnp.bfloat16),
            pltpu.VMEM((2, blocks, cols, half, pool_rows), jnp.float32),
            pltpu.VMEM((2, blocks, half, pool_rows), jnp.float32),
            pltpu.SemaphoreType.DMA((sends,)),
            pltpu.SemaphoreType.DMA((4, blocks)),
            pltpu.SemaphoreType.DMA((6,)),
            pltpu.SemaphoreType.DMA((2,)),
            pltpu.SemaphoreType.DMA((2,)),
        ],
        compiler_params=pltpu.CompilerParams(
            collective_id=0, has_side_effects=True, vmem_limit_bytes=48 * 2**20
        ),
    )(pool_acts, pool_grads, label_acts, label_grads)
    return out.reshape(pool_rows, 1, blocks * half)


def solution(mesh):
    placed = (
        P(("groups", "rows"), "cols"),
        P(("groups", "rows"), "cols"),
        P(("groups", "rows"), "cols"),
        P(("groups", "rows"), "cols"),
    )
    return jax.shard_map(
        body,
        mesh=mesh,
        in_specs=placed,
        out_specs=P(("groups", "rows"), "cols", None),
        check_vma=False,
    )
```

```python
import functools

import jax
import jax.numpy as jnp
from jax import lax
from jax.experimental import pallas as pl
from jax.experimental.pallas import tpu as pltpu
from jax.sharding import PartitionSpec as P

MESH = pl.DeviceIdType.MESH
ORDERS = ((0, 2, 1), (0, 1, 2), (2, 0, 1), (1, 0, 2))
LANES = 128


def contract(left, right):
    return lax.dot_general(
        left, right, (((1,), (1,)), ((), ())), preferred_element_type=jnp.float32
    )


def kernel(
    sizes, spans,
    pool_acts, pool_grads, label_acts, label_grads, out_ref,
    buf0, buf1, buf2, buf3, acts, grads, gram, other,
    send_sem, recv_sem, local_sem, pair_send, pair_recv,
):
    bufs = (buf0, buf1, buf2, buf3)
    me = lax.axis_index("rows")
    core = lax.axis_index("cols")
    strides = (sizes[1] * sizes[2], sizes[2], 1)
    place = [lax.rem(me // s, n) for s, n in zip(strides, sizes)]
    blocks = sizes[0] * sizes[1] * sizes[2]

    def at(delta):
        return sum(
            lax.rem(place[a] + delta[a], sizes[a]) * strides[a] for a in range(3)
        )

    def along(axis):
        return [
            tuple(d if a == axis else 0 for a in range(3))
            for d in range(1, sizes[axis])
        ]

    barrier = pltpu.get_barrier_semaphore()
    greeted = 1
    pl.semaphore_signal(
        barrier, inc=1, device_id={"cols": 1 - core}, device_id_type=MESH
    )
    for axis in range(3):
        for peer in along(axis):
            pl.semaphore_signal(
                barrier, inc=1, device_id={"rows": at(peer)}, device_id_type=MESH
            )
            greeted += 1
    pl.semaphore_wait(barrier, greeted)

    own = [label_acts if s is None else label_grads.at[:, s[0] : s[1]] for s in spans]
    sent = []

    def send(k, delta, peer):
        block = at(delta)
        src = bufs[k].at[block] if any(delta) else own[k]
        copy = pltpu.make_async_remote_copy(
            src_ref=src,
            dst_ref=bufs[k].at[block],
            send_sem=send_sem.at[len(sent)],
            recv_sem=recv_sem.at[k, block],
            device_id={"rows": at(peer)},
            device_id_type=MESH,
        )
        copy.start()
        sent.append(copy)

    def arrived(k, delta):
        block = at(delta)
        pltpu.make_async_remote_copy(
            src_ref=bufs[k].at[block],
            dst_ref=bufs[k].at[block],
            send_sem=send_sem.at[0],
            recv_sem=recv_sem.at[k, block],
            device_id={"rows": at(along(2)[0])},
            device_id_type=MESH,
        ).wait_recv()

    def plus(*deltas):
        return tuple(sum(d) for d in zip(*deltas))

    zero = (0, 0, 0)
    for leg in range(3):
        for k, order in enumerate(ORDERS):
            for peer in along(order[leg]):
                send(k, zero, peer)

    local = [
        pltpu.make_async_copy(own[k], bufs[k].at[me], local_sem.at[k])
        for k in range(4)
    ]
    local.append(pltpu.make_async_copy(pool_acts, acts, local_sem.at[4]))
    local.append(pltpu.make_async_copy(pool_grads, grads, local_sem.at[5]))
    for copy in local:
        copy.start()

    for step in range(max(sizes) - 1):
        for k, order in enumerate(ORDERS):
            first = along(order[0])
            if step < len(first):
                arrived(k, first[step])
                for leg in (1, 2):
                    for peer in along(order[leg]):
                        send(k, first[step], peer)

    second = [
        [plus(f, s) for f in [zero] + along(o[0]) for s in along(o[1])]
        for o in ORDERS
    ]
    for step in range(max(len(s) for s in second)):
        for k, order in enumerate(ORDERS):
            if step < len(second[k]):
                arrived(k, second[k][step])
                for peer in along(order[2]):
                    send(k, second[k][step], peer)

    third = [
        [
            plus(f, s, t)
            for f in [zero] + along(o[0])
            for s in [zero] + along(o[1])
            for t in along(o[2])
        ]
        for o in ORDERS
    ]

    def pair(which):
        return pltpu.make_async_remote_copy(
            src_ref=gram.at[which, :, 1 - core],
            dst_ref=other.at[which],
            send_sem=pair_send.at[which],
            recv_sem=pair_recv.at[which],
            device_id={"cols": 1 - core},
            device_id_type=MESH,
        )

    def flat(k):
        return bufs[k][...].reshape(blocks * bufs[k].shape[1], bufs[k].shape[2])

    for copy in local:
        copy.wait()
    for delta in third[0]:
        arrived(0, delta)
    gram[0] = contract(flat(0), acts[...]).reshape(gram.shape[1:])
    pair(0).start()
    for k in (1, 2, 3):
        for delta in third[k]:
            arrived(k, delta)
    total = None
    for k in (1, 2, 3):
        part = contract(flat(k), grads[:, spans[k][0] : spans[k][1]])
        total = part if total is None else total + part
    gram[1] = total.reshape(gram.shape[1:])
    pair(1).start()
    pair(0).wait()
    pair(1).wait()
    result = (gram[0, :, core] + other[0]) * (gram[1, :, core] + other[1])
    out_ref[...] = result.reshape(out_ref.shape[1], out_ref.shape[0]).T
    for copy in sent:
        copy.wait_send()


def body(pool_acts, pool_grads, label_acts, label_grads):
    blocks = lax.axis_size("rows")
    cols = lax.axis_size("cols")
    sizes = (blocks // 4, 2, 2)
    pool_rows = pool_acts.shape[0]
    block_rows = label_acts.shape[0]
    half = block_rows // cols
    wide = label_grads.shape[1]
    quarter = wide // 4
    spans = (None, (0, 2 * quarter), (2 * quarter, 3 * quarter), (3 * quarter, wide))
    widths = (label_acts.shape[1], 2 * quarter, quarter, wide - 3 * quarter)
    sends = 0
    for o in ORDERS:
        n = [sizes[a] for a in o]
        sends += (n[0] - 1) + n[0] * (n[1] - 1) + n[0] * n[1] * (n[2] - 1)
    out = pl.pallas_call(
        functools.partial(kernel, sizes, spans),
        out_shape=jax.ShapeDtypeStruct((pool_rows, blocks * half), jnp.float32),
        in_specs=[pl.BlockSpec(memory_space=pltpu.HBM)] * 4,
        out_specs=pl.BlockSpec(memory_space=pltpu.VMEM),
        scratch_shapes=[
            pltpu.VMEM((blocks, block_rows, w), jnp.bfloat16) for w in widths
        ]
        + [
            pltpu.VMEM(pool_acts.shape, jnp.bfloat16),
            pltpu.VMEM(pool_grads.shape, jnp.bfloat16),
            pltpu.VMEM((2, blocks, cols, half, pool_rows), jnp.float32),
            pltpu.VMEM((2, blocks, half, pool_rows), jnp.float32),
            pltpu.SemaphoreType.DMA((sends,)),
            pltpu.SemaphoreType.DMA((4, blocks)),
            pltpu.SemaphoreType.DMA((6,)),
            pltpu.SemaphoreType.DMA((2,)),
            pltpu.SemaphoreType.DMA((2,)),
        ],
        compiler_params=pltpu.CompilerParams(
            collective_id=0, has_side_effects=True, vmem_limit_bytes=63 * 2**20
        ),
    )(pool_acts, pool_grads, label_acts, label_grads)
    return out.reshape(pool_rows, 1, blocks * half)


def solution(mesh):
    placed = (
        P(("groups", "rows"), "cols"),
        P(("groups", "rows"), "cols"),
        P(("groups", "rows"), "cols"),
        P(("groups", "rows"), "cols"),
    )
    return jax.shard_map(
        body,
        mesh=mesh,
        in_specs=placed,
        out_specs=P(("groups", "rows"), "cols", None),
        check_vma=False,
    )
```

```python
import functools

import jax
import jax.numpy as jnp
from jax import lax
from jax.experimental import pallas as pl
from jax.experimental.pallas import tpu as pltpu
from jax.sharding import PartitionSpec as P

MESH = pl.DeviceIdType.MESH
ORDERS = ((0, 2, 1), (0, 1, 2), (2, 0, 1), (1, 0, 2))
LANES = 128


def contract(left, right):
    return lax.dot_general(
        left, right, (((1,), (1,)), ((), ())), preferred_element_type=jnp.float32
    )


def kernel(
    sizes, spans,
    pool_acts, pool_grads, label_acts, label_grads, out_ref,
    buf0, buf1, buf2, buf3, acts, grads, gram, other,
    send_sem, recv_sem, local_sem, pair_send, pair_recv,
):
    bufs = (buf0, buf1, buf2, buf3)
    me = lax.axis_index("rows")
    core = lax.axis_index("cols")
    strides = (sizes[1] * sizes[2], sizes[2], 1)
    place = [lax.rem(me // s, n) for s, n in zip(strides, sizes)]
    blocks = sizes[0] * sizes[1] * sizes[2]

    def flip(value, bits):
        out, bit = 0, 1
        while bit < max(sizes):
            out += lax.rem(value // bit + bits // bit, 2) * bit
            bit *= 2
        return out

    def at(delta):
        return sum(flip(place[a], delta[a]) * strides[a] for a in range(3))

    def along(axis):
        return [
            tuple(d if a == axis else 0 for a in range(3))
            for d in range(1, sizes[axis])
        ]

    own = [label_acts if s is None else label_grads.at[:, s[0] : s[1]] for s in spans]
    local = [
        pltpu.make_async_copy(own[k], bufs[k].at[me], local_sem.at[k])
        for k in range(4)
    ]
    local.append(pltpu.make_async_copy(pool_acts, acts, local_sem.at[4]))
    local.append(pltpu.make_async_copy(pool_grads, grads, local_sem.at[5]))
    for copy in local:
        copy.start()

    barrier = pltpu.get_barrier_semaphore()
    greeted = 1
    pl.semaphore_signal(
        barrier, inc=1, device_id={"cols": 1 - core}, device_id_type=MESH
    )
    for axis in range(3):
        for peer in along(axis):
            pl.semaphore_signal(
                barrier, inc=1, device_id={"rows": at(peer)}, device_id_type=MESH
            )
            greeted += 1
    pl.semaphore_wait(barrier, greeted)
    for copy in local[:4]:
        copy.wait()

    sent = []

    def send(k, delta, peer):
        block = at(delta)
        copy = pltpu.make_async_remote_copy(
            src_ref=bufs[k].at[block],
            dst_ref=bufs[k].at[block],
            send_sem=send_sem.at[len(sent)],
            recv_sem=recv_sem.at[k, block],
            device_id={"rows": at(peer)},
            device_id_type=MESH,
        )
        copy.start()
        sent.append(copy)

    def arrived(k, delta):
        block = at(delta)
        pltpu.make_async_remote_copy(
            src_ref=bufs[k].at[block],
            dst_ref=bufs[k].at[block],
            send_sem=send_sem.at[0],
            recv_sem=recv_sem.at[k, block],
            device_id={"rows": at(along(2)[0])},
            device_id_type=MESH,
        ).wait_recv()

    def plus(*deltas):
        return tuple(functools.reduce(lambda p, q: p ^ q, d) for d in zip(*deltas))

    zero = (0, 0, 0)
    for leg in range(3):
        for k, order in enumerate(ORDERS):
            for peer in along(order[leg]):
                send(k, zero, peer)

    passed = []
    for k, order in enumerate(ORDERS):
        for f in [zero] + along(order[0]):
            if any(f):
                passed.append((k, f, (1, 2)))
            for s in along(order[1]):
                passed.append((k, plus(f, s), (2,)))
    passed.sort(key=lambda e: ((-len(e[2]), sum(d.bit_length() for d in e[1]))))
    for k, delta, legs in passed:
        arrived(k, delta)
        for leg in legs:
            for peer in along(ORDERS[k][leg]):
                send(k, delta, peer)

    third = [
        [
            plus(f, s, t)
            for f in [zero] + along(o[0])
            for s in [zero] + along(o[1])
            for t in along(o[2])
        ]
        for o in ORDERS
    ]

    def pair(which):
        return pltpu.make_async_remote_copy(
            src_ref=gram.at[which, :, 1 - core],
            dst_ref=other.at[which],
            send_sem=pair_send.at[which],
            recv_sem=pair_recv.at[which],
            device_id={"cols": 1 - core},
            device_id_type=MESH,
        )

    def flat(k):
        return bufs[k][...].reshape(blocks * bufs[k].shape[1], bufs[k].shape[2])

    for copy in local[4:]:
        copy.wait()
    for delta in third[0]:
        arrived(0, delta)
    gram[0] = contract(flat(0), acts[...]).reshape(gram.shape[1:])
    pair(0).start()
    for k in (1, 2, 3):
        for delta in third[k]:
            arrived(k, delta)
    total = None
    for k in (1, 2, 3):
        part = contract(flat(k), grads[:, spans[k][0] : spans[k][1]])
        total = part if total is None else total + part
    gram[1] = total.reshape(gram.shape[1:])
    pair(1).start()
    pair(0).wait()
    pair(1).wait()
    result = (gram[0, :, core] + other[0]) * (gram[1, :, core] + other[1])
    out_ref[...] = result.reshape(out_ref.shape[1], out_ref.shape[0]).T
    for copy in sent:
        copy.wait_send()


def body(pool_acts, pool_grads, label_acts, label_grads):
    blocks = lax.axis_size("rows")
    cols = lax.axis_size("cols")
    sizes = (blocks // 4, 2, 2)
    pool_rows = pool_acts.shape[0]
    block_rows = label_acts.shape[0]
    half = block_rows // cols
    wide = label_grads.shape[1]
    quarter = wide // 4
    spans = (None, (0, 2 * quarter), (2 * quarter, 3 * quarter), (3 * quarter, wide))
    widths = (label_acts.shape[1], 2 * quarter, quarter, wide - 3 * quarter)
    sends = 0
    for o in ORDERS:
        n = [sizes[a] for a in o]
        sends += (n[0] - 1) + n[0] * (n[1] - 1) + n[0] * n[1] * (n[2] - 1)
    out = pl.pallas_call(
        functools.partial(kernel, sizes, spans),
        out_shape=jax.ShapeDtypeStruct((pool_rows, blocks * half), jnp.float32),
        in_specs=[pl.BlockSpec(memory_space=pltpu.HBM)] * 4,
        out_specs=pl.BlockSpec(memory_space=pltpu.VMEM),
        scratch_shapes=[
            pltpu.VMEM((blocks, block_rows, w), jnp.bfloat16) for w in widths
        ]
        + [
            pltpu.VMEM(pool_acts.shape, jnp.bfloat16),
            pltpu.VMEM(pool_grads.shape, jnp.bfloat16),
            pltpu.VMEM((2, blocks, cols, half, pool_rows), jnp.float32),
            pltpu.VMEM((2, blocks, half, pool_rows), jnp.float32),
            pltpu.SemaphoreType.DMA((sends,)),
            pltpu.SemaphoreType.DMA((4, blocks)),
            pltpu.SemaphoreType.DMA((6,)),
            pltpu.SemaphoreType.DMA((2,)),
            pltpu.SemaphoreType.DMA((2,)),
        ],
        compiler_params=pltpu.CompilerParams(
            collective_id=0, has_side_effects=True, vmem_limit_bytes=63 * 2**20
        ),
    )(pool_acts, pool_grads, label_acts, label_grads)
    return out.reshape(pool_rows, 1, blocks * half)


def solution(mesh):
    placed = (
        P(("groups", "rows"), "cols"),
        P(("groups", "rows"), "cols"),
        P(("groups", "rows"), "cols"),
        P(("groups", "rows"), "cols"),
    )
    return jax.shard_map(
        body,
        mesh=mesh,
        in_specs=placed,
        out_specs=P(("groups", "rows"), "cols", None),
        check_vma=False,
    )
```

```python
import functools

import jax
import jax.numpy as jnp
from jax import lax
from jax.experimental import pallas as pl
from jax.experimental.pallas import tpu as pltpu
from jax.sharding import PartitionSpec as P

MESH = pl.DeviceIdType.MESH
ORDERS = ((0, 2, 1), (0, 1, 2), (2, 0, 1), (1, 0, 2))
LANES = 128


def contract(left, right):
    return lax.dot_general(
        left, right, (((1,), (1,)), ((), ())), preferred_element_type=jnp.float32
    )


def kernel(
    sizes, spans,
    pool_acts, pool_grads, label_acts, label_grads, out_ref,
    buf0, buf1, buf2, buf3, acts, grads, gram, other,
    send_sem, recv_sem, local_sem, pair_send, pair_recv,
):
    bufs = (buf0, buf1, buf2, buf3)
    me = lax.axis_index("rows")
    core = lax.axis_index("cols")
    strides = (sizes[1] * sizes[2], sizes[2], 1)
    place = [lax.rem(me // s, n) for s, n in zip(strides, sizes)]
    blocks = sizes[0] * sizes[1] * sizes[2]

    def flip(value, bits):
        out, bit = 0, 1
        while bit < max(sizes):
            out += lax.rem(value // bit + bits // bit, 2) * bit
            bit *= 2
        return out

    def spot(delta):
        return tuple(flip(place[a], delta[a]) for a in range(3))

    def at(delta):
        return sum(p * s for p, s in zip(spot(delta), strides))

    def along(axis):
        return [
            tuple(d if a == axis else 0 for a in range(3))
            for d in range(1, sizes[axis])
        ]

    own = [label_acts if s is None else label_grads.at[:, s[0] : s[1]] for s in spans]
    local = [
        pltpu.make_async_copy(own[k], bufs[k].at[tuple(place)], local_sem.at[k])
        for k in range(4)
    ]
    local.append(pltpu.make_async_copy(pool_acts, acts, local_sem.at[4]))
    local.append(pltpu.make_async_copy(pool_grads, grads, local_sem.at[5]))
    for copy in local:
        copy.start()

    gram[...] = jnp.zeros_like(gram)
    barrier = pltpu.get_barrier_semaphore()
    greeted = 1
    pl.semaphore_signal(
        barrier, inc=1, device_id={"cols": 1 - core}, device_id_type=MESH
    )
    for axis in range(3):
        for peer in along(axis):
            pl.semaphore_signal(
                barrier, inc=1, device_id={"rows": at(peer)}, device_id_type=MESH
            )
            greeted += 1
    pl.semaphore_wait(barrier, greeted)
    for copy in local[:4]:
        copy.wait()

    sent = []

    def send(k, delta, peer):
        block = at(delta)
        copy = pltpu.make_async_remote_copy(
            src_ref=bufs[k].at[spot(delta)],
            dst_ref=bufs[k].at[spot(delta)],
            send_sem=send_sem.at[len(sent)],
            recv_sem=recv_sem.at[k, block],
            device_id={"rows": at(peer)},
            device_id_type=MESH,
        )
        copy.start()
        sent.append(copy)

    def arrived(k, delta):
        block = at(delta)
        pltpu.make_async_remote_copy(
            src_ref=bufs[k].at[spot(delta)],
            dst_ref=bufs[k].at[spot(delta)],
            send_sem=send_sem.at[0],
            recv_sem=recv_sem.at[k, block],
            device_id={"rows": at(along(2)[0])},
            device_id_type=MESH,
        ).wait_recv()

    def plus(*deltas):
        return tuple(functools.reduce(lambda p, q: p ^ q, d) for d in zip(*deltas))

    zero = (0, 0, 0)
    for leg in range(3):
        for k, order in enumerate(ORDERS):
            for peer in along(order[leg]):
                send(k, zero, peer)

    passed = []
    for k, order in enumerate(ORDERS):
        for f in [zero] + along(order[0]):
            if any(f):
                passed.append((k, f, (1, 2)))
            for s in along(order[1]):
                passed.append((k, plus(f, s), (2,)))
    passed.sort(key=lambda e: ((-len(e[2]), sum(d.bit_length() for d in e[1]))))
    for k, delta, legs in passed:
        arrived(k, delta)
        for leg in legs:
            for peer in along(ORDERS[k][leg]):
                send(k, delta, peer)

    third = [
        [
            plus(f, s, t)
            for f in [zero] + along(o[0])
            for s in [zero] + along(o[1])
            for t in along(o[2])
        ]
        for o in ORDERS
    ]

    def pair(which):
        return pltpu.make_async_remote_copy(
            src_ref=gram.at[which, :, :, :, 1 - core],
            dst_ref=other.at[which],
            send_sem=pair_send.at[which],
            recv_sem=pair_recv.at[which],
            device_id={"cols": 1 - core},
            device_id_type=MESH,
        )

    def add(k, late):
        axis = ORDERS[k][2]
        side = lax.rem(place[axis] + late, 2)
        part = (slice(None),) * axis + (side,)
        which, pool = (0, acts) if k == 0 else (1, grads)
        rows = bufs[k][part]
        rows = rows.reshape(-1, rows.shape[-1])
        span = slice(None) if k == 0 else slice(*spans[k])
        target = gram.at[(which,) + part]
        target[...] += contract(rows, pool[:, span]).reshape(target.shape)

    for copy in local[4:]:
        copy.wait()
    for k in range(4):
        add(k, 0)
    for k in range(4):
        for delta in third[k]:
            arrived(k, delta)
        add(k, 1)
        if k == 0:
            pair(0).start()
    pair(1).start()
    pair(0).wait()
    pair(1).wait()
    result = (gram[0, :, :, :, core] + other[0]) * (gram[1, :, :, :, core] + other[1])
    out_ref[...] = result.reshape(out_ref.shape[1], out_ref.shape[0]).T
    for copy in sent:
        copy.wait_send()


def body(pool_acts, pool_grads, label_acts, label_grads):
    blocks = lax.axis_size("rows")
    cols = lax.axis_size("cols")
    sizes = (blocks // 4, 2, 2)
    pool_rows = pool_acts.shape[0]
    block_rows = label_acts.shape[0]
    half = block_rows // cols
    wide = label_grads.shape[1]
    quarter = wide // 4
    spans = (None, (0, 1152), (1152, 1536), (1536, wide))
    widths = (label_acts.shape[1], 1152, 384, 512)
    sends = 0
    for o in ORDERS:
        n = [sizes[a] for a in o]
        sends += (n[0] - 1) + n[0] * (n[1] - 1) + n[0] * n[1] * (n[2] - 1)
    out = pl.pallas_call(
        functools.partial(kernel, sizes, spans),
        out_shape=jax.ShapeDtypeStruct((pool_rows, blocks * half), jnp.float32),
        in_specs=[pl.BlockSpec(memory_space=pltpu.HBM)] * 4,
        out_specs=pl.BlockSpec(memory_space=pltpu.VMEM),
        scratch_shapes=[
            pltpu.VMEM((*sizes, block_rows, w), jnp.bfloat16) for w in widths
        ]
        + [
            pltpu.VMEM(pool_acts.shape, jnp.bfloat16),
            pltpu.VMEM(pool_grads.shape, jnp.bfloat16),
            pltpu.VMEM((2, *sizes, cols, half, pool_rows), jnp.float32),
            pltpu.VMEM((2, *sizes, half, pool_rows), jnp.float32),
            pltpu.SemaphoreType.DMA((sends,)),
            pltpu.SemaphoreType.DMA((4, blocks)),
            pltpu.SemaphoreType.DMA((6,)),
            pltpu.SemaphoreType.DMA((2,)),
            pltpu.SemaphoreType.DMA((2,)),
        ],
        compiler_params=pltpu.CompilerParams(
            collective_id=0, has_side_effects=True, vmem_limit_bytes=63 * 2**20
        ),
    )(pool_acts, pool_grads, label_acts, label_grads)
    return out.reshape(pool_rows, 1, blocks * half)


def solution(mesh):
    placed = (
        P(("groups", "rows"), "cols"),
        P(("groups", "rows"), "cols"),
        P(("groups", "rows"), "cols"),
        P(("groups", "rows"), "cols"),
    )
    return jax.shard_map(
        body,
        mesh=mesh,
        in_specs=placed,
        out_specs=P(("groups", "rows"), "cols", None),
        check_vma=False,
    )
```
